32 devices in a mesh: comp: 2 (over core), lat: 4 (over z), lon: 4 (over y, x).
Axes of the slice: x: 2, y: 2, z: 4, core: 2. Of those that a mesh axis runs over, the one named last changes fastest.
Arguments:
- state_field: bfloat16 [2, 128, 128, 768], P('comp', 'lat', 'lon'), may hold values from -8 to 8
- sea_mask: int32 [128, 128], P('lat', 'lon'), may hold values from 0 to 1, as said below
- w_qkv: bfloat16 [768, 2304], replicated, may hold values from -1 to 1
- w_attn_out: bfloat16 [768, 768], replicated, may hold values from -0.21875 to 0.21875
- w_up: bfloat16 [768, 3072], replicated, may hold values from -0.21875 to 0.21875
- w_down: bfloat16 [3072, 768], replicated, may hold values from -0.109375 to 0.109375
- conv_weight: bfloat16 [4, 3, 3, 128, 128], replicated, may hold values from -0.1875 to 0.1875
- conv_bias: float32 [4, 128], replicated, may hold values from -3 to 3
- w_surface: bfloat16 [2, 768, 256], P('comp'), may hold values from -0.21875 to 0.21875
- w_forcing: bfloat16 [2, 256, 768], P('comp'), may hold values from -0.375 to 0.375
- regrid_blocks: bfloat16 [2, 4, 256, 256], replicated, may hold values from -0.375 to 0.375
- routes: int32 [2, 4, 4, 1024, 2], P('comp', 'lat', 'lon'), may hold values from 0 to 15, all different within a row; in each aligned block of 1024 rows (0 to 1023, 1024 to 2047, ..., all dimensions but the last counted through in order) at most 192 rows name the same one
- dest_entry: int32 [2, 4, 4, 1024, 2], P('comp', 'lat', 'lon'), may hold values from 0 to 1023
- block_index: int32 [2, 4, 4, 1024, 2], P('comp', 'lat', 'lon'), may hold values from 0 to 3
Outputs:
- new_field: bfloat16 [2, 128, 128, 768], P('comp', 'lat', 'lon')
The draws below stay inside these ranges and needn't reach their ends.
Inputs may be any that keep to these rules, and one draw needn't show every extreme that they name: `sea_mask`: 1 marks sea and 0 land; the share of land is drawn anew for each band of 32 rows. routes[c, i, j, e, t] numbers the device of component 1 - c that link t of entry e of device (i, j) feeds; the 2 links of an entry name different devices; the entries of one device name one destination at most 192 times, a bound that some block reaches. `dest_entry`: the destination entry, row-major within the destination device's block. `block_index`: the sending component's regridding block that the link applies.
All inputs are finite; a program needn't handle non-finite values.
Results may differ from the reference program's by a relative error of at most 0.007.
Values may be sent and summed in bfloat16 or wider, within the bound.
A program may use at most 192 MiB of HBM per device.

```python
import math
import jax
import jax.numpy as jnp
import numpy as np
from jax import lax

D = 768
HEAD = 64
HID = 3072
OCH = 128
PACK = 6
SFEAT = 256
NBLK = 4
WIN = 8
OLAY = 4
TOP = 2
ROWS = 32
COLS = 32
ENTRY = 1024
GROUP = 16
CAP = 192
NR = 128
NC = 128
N_LAT = 4
N_LON = 4


def draw_state_field(key, part):
    base_key = jax.random.fold_in(key, 0)
    normal_draw = jax.random.normal(base_key, (2, NR, NC, D), jnp.float32)
    return jnp.clip(normal_draw, -8.0, 8.0).astype(jnp.bfloat16)


def draw_sea_mask(key, part):
    band_key, cell_key = jax.random.split(key)
    land_share = jax.random.randint(band_key, (NR // ROWS, 1), 5, 90)
    land_share = jnp.repeat(land_share, ROWS, axis=0)
    dice_roll = jax.random.randint(cell_key, (NR, NC), 0, 100)
    return (dice_roll >= land_share).astype(jnp.int32)


def draw_w_qkv(key, part):
    shared_key = jax.random.fold_in(key, 0)
    full_matrix = jnp.clip(jax.random.normal(shared_key, (D, 3 * D), jnp.float32), -6.0, 6.0) / math.sqrt(D)
    return jnp.clip(full_matrix, -1.0, 1.0).astype(jnp.bfloat16)


def touch_ends(entries, key, least, high):
    longest = entries.shape.index(max(entries.shape))
    spots = []
    for shift in (0, 1):
        where = [jax.random.randint(jax.random.fold_in(key, axis), (), 0, length) for axis, length in enumerate(entries.shape)]
        where[longest] = (where[longest] + shift) % entries.shape[longest]
        spots.append(tuple(where))
    return entries.at[spots[0]].set(least).at[spots[1]].set(high)


def level_of(own_key, dims, cuts, smallest, high):
    level, own = 1.0, jax.random.fold_in(own_key, 6)
    for dim, parts in cuts:
        draws = jnp.exp(jax.random.uniform(jax.random.fold_in(own, dim), (parts,), jnp.float32, smallest / len(cuts), high / len(cuts)))
        level = level * jnp.repeat(draws, dims[dim] // parts).reshape([-1 if axis == dim else 1 for axis in range(len(dims))])
    return level


def routed_block(own_key, own, number, rows, count, top, limit, slope):
    order = jax.random.permutation(own_key, count)
    crowded, usual = shares(count, rows * top, limit, slope, True), shares(count, rows * top, limit, slope, False)
    places = jnp.arange(count)

    def named(tallies, turn):
        used = int((tallies > 0).sum())
        fixed = max(1, used // 4)
        shifted = fixed + (places - fixed + turn * (used - fixed)) % max(1, count - fixed)
        return jnp.zeros((count,), jnp.int32).at[order[jnp.where(places < fixed, places, shifted)]].set(jnp.asarray(tallies, jnp.int32))

    tallies = jnp.where(number % 4 == 0, named(crowded, number // 4), named(usual, number - number // 4 - 1))
    mixed = jax.random.permutation(jax.random.fold_in(own, 3), count)
    donor, sink = mixed[0:count // 2 * 2:2], mixed[1:count // 2 * 2:2]
    room = jnp.minimum(tallies[donor] - 1, limit - tallies[sink]) // 2
    room = jnp.where((donor == order[0]) | (sink == order[0]) | (tallies[sink] == 0), 0, jnp.maximum(room, 0))
    shifted = jax.random.randint(jax.random.fold_in(own, 4), (count // 2,), 0, 1 << 20) % (room + 1)
    tallies = tallies.at[donor].add(-shifted).at[sink].add(shifted)
    members = jnp.searchsorted(jnp.cumsum(tallies), jnp.arange(rows * top), side="right").astype(jnp.int32)
    grid = members.reshape(top, rows).T
    grid = grid[jax.random.permutation(jax.random.fold_in(own, 1), rows)]
    turn = jax.random.randint(jax.random.fold_in(own, 2), (rows, 1), 0, top)
    return jnp.take_along_axis(grid, (jnp.arange(top)[None, :] + turn) % top, axis=1)


def shares(amount, total, most, slope, full):
    portions = [(1 << 20) // math.isqrt(rank ** slope) + 1 for rank in range(1, amount + 1)]
    largest = most if full else min(most, max(-(-total // amount), total * portions[0] // sum(portions)))
    least = 1 if total - largest >= amount - 1 else 0
    counts, surplus = [largest] + [least] * (amount - 1), total - largest - least * (amount - 1)
    while surplus > 0:
        free = [i for i in range(1, amount) if counts[i] < largest] or [i for i in range(1, amount) if counts[i] < most]
        pool, remaining = sum([portions[i] for i in free]), surplus
        for i in free:
            extra = min(most - counts[i], max(1, remaining * portions[i] // pool), surplus)
            counts[i] = counts[i] + extra
            surplus = surplus - extra
    return np.array(counts)


def bell_draw(rng, extent, scale, most, cuts=(), kind=jnp.bfloat16):
    result = scale * jax.random.normal(rng, extent, jnp.float32)
    if cuts:
        result = result * level_of(rng, extent, cuts, -0.22, 0.18)
    return jnp.clip(result, -most, most).astype(kind)


def setup_inputs(seed: int = 0) -> dict:
    arg_keys = jax.random.split(jax.random.key(seed), 15)
    state_field = draw_state_field(jax.random.fold_in(arg_keys[14], 71), 0)
    sea_mask = draw_sea_mask(jax.random.fold_in(arg_keys[14], 71), 0)
    w_qkv = draw_w_qkv(jax.random.fold_in(arg_keys[14], 71), 0)
    w_attn_out = bell_draw(arg_keys[3], (D, D), D ** -0.5, 0.21875)
    w_up = bell_draw(arg_keys[4], (D, HID), D ** -0.5, 0.21875)
    w_down = bell_draw(arg_keys[5], (HID, D), HID ** -0.5, 0.109375)
    conv_weight = bell_draw(arg_keys[6], (OLAY, 3, 3, OCH, OCH), (9 * OCH) ** -0.5, 0.1875)
    conv_bias = bell_draw(arg_keys[7], (OLAY, OCH), 0.5, 3.0, (), jnp.float32)
    w_surface = bell_draw(arg_keys[8], (2, D, SFEAT), D ** -0.5, 0.21875, ((0, 2),))
    w_forcing = bell_draw(arg_keys[9], (2, SFEAT, D), SFEAT ** -0.5, 0.375, ((0, 2),))
    regrid_blocks = bell_draw(arg_keys[10], (2, NBLK, SFEAT, SFEAT), SFEAT ** -0.5, 0.375)
    routes_keys = jax.random.split(jax.random.fold_in(arg_keys[11], 1), 2 * N_LAT * N_LON * ENTRY // ENTRY)
    routes_turns = jax.random.permutation(jax.random.fold_in(arg_keys[11], 3), 2 * N_LAT * N_LON * ENTRY // ENTRY)
    routes = jax.vmap(lambda own, number: routed_block(jax.random.fold_in(arg_keys[11], 2), own, number, ENTRY, GROUP, TOP, CAP, 2))(routes_keys, routes_turns).reshape((2, N_LAT, N_LON, ENTRY, TOP))
    dest_entry = touch_ends(jax.random.randint(arg_keys[12], (2, N_LAT, N_LON, ENTRY, TOP), 0, ENTRY), jax.random.fold_in(arg_keys[12], 1), 0, ENTRY - 1).astype(jnp.int32)
    block_index = touch_ends(jax.random.randint(arg_keys[13], (2, N_LAT, N_LON, ENTRY, TOP), 0, NBLK), jax.random.fold_in(arg_keys[13], 1), 0, NBLK - 1).astype(jnp.int32)
    return dict(state_field=state_field, sea_mask=sea_mask, w_qkv=w_qkv, w_attn_out=w_attn_out, w_up=w_up, w_down=w_down, conv_weight=conv_weight, conv_bias=conv_bias, w_surface=w_surface, w_forcing=w_forcing, regrid_blocks=regrid_blocks, routes=routes, dest_entry=dest_entry, block_index=block_index)


EPSILON = 1e-05

def normalize(values):
    average = lax.optimization_barrier(jnp.mean(values, axis=-1, keepdims=True))
    centred = values - average
    spread = lax.optimization_barrier(jnp.mean(centred * centred, axis=-1, keepdims=True))
    return centred * lax.rsqrt(spread + EPSILON)

def blocked(cell_grid):
    feature_width = cell_grid.shape[-1]
    moved = cell_grid.reshape(N_LAT, ROWS, N_LON, COLS, feature_width).transpose(0, 2, 1, 3, 4)
    return moved.reshape(GROUP * ENTRY, feature_width)

def unblocked(flat_rows):
    feature_width = flat_rows.shape[-1]
    moved = flat_rows.reshape(N_LAT, N_LON, ROWS, COLS, feature_width).transpose(0, 2, 1, 3, 4)
    return moved.reshape(NR, NC, feature_width)

def atmosphere_core(tokens, w_qkv, w_attn_out, w_up, w_down):
    margin = WIN // 2
    head_count = D // HEAD
    padded = jnp.pad(tokens, ((margin, margin), (0, 0), (0, 0)))
    extended = jnp.concatenate([padded[:, NC - margin:], padded, padded[:, :margin]], axis=1)
    ext_cols = NC + 2 * margin
    win_cols = ext_cols // WIN
    win_rows = (NR + 2 * margin) // WIN

    def window_row(row_block):
        band_rows = lax.dynamic_slice_in_dim(extended, (row_block * WIN).astype(jnp.int32), WIN, 0)
        normed = normalize(band_rows.astype(jnp.float32)).astype(jnp.bfloat16)
        packed = jnp.dot(normed.reshape(-1, D), w_qkv, preferred_element_type=jnp.float32).astype(jnp.bfloat16)
        packed = packed.reshape(WIN, win_cols, WIN, 3, head_count, HEAD).transpose(1, 0, 2, 3, 4, 5)
        packed = packed.reshape(win_cols, WIN * WIN, 3, head_count, HEAD).astype(jnp.float32)
        scores = jnp.einsum('nqhd,nkhd->nhqk', packed[:, :, 0], packed[:, :, 1]) * HEAD ** (-0.5)
        positions = row_block * WIN - margin + jnp.arange(WIN, dtype=jnp.int32)
        inside = (positions >= 0) & (positions < NR)
        key_ok = jnp.repeat(inside, WIN)
        scores = jnp.where(key_ok[None, None, None, :], scores, -jnp.inf)
        largest = lax.optimization_barrier(jnp.max(scores, axis=-1, keepdims=True))
        exponent = jnp.exp(scores - largest)
        weights = (exponent / lax.optimization_barrier(jnp.sum(exponent, axis=-1, keepdims=True))).astype(jnp.bfloat16)
        attended = jnp.einsum('nhqk,nkhd->nqhd', weights.astype(jnp.float32), packed[:, :, 2]).astype(jnp.bfloat16)
        return attended.reshape(win_cols, WIN, WIN, D).transpose(1, 0, 2, 3).reshape(WIN, ext_cols, D)
    attended = lax.map(window_row, jnp.arange(win_rows, dtype=jnp.int32))
    attended = attended.reshape(win_rows * WIN, ext_cols, D)[margin:margin + NR, margin:margin + NC]
    projected = jnp.dot(attended.reshape(-1, D), w_attn_out, preferred_element_type=jnp.float32)
    first_sum = (tokens.reshape(-1, D).astype(jnp.float32) + projected).astype(jnp.bfloat16)
    normed_two = normalize(first_sum.astype(jnp.float32)).astype(jnp.bfloat16)
    hidden = jax.nn.gelu(jnp.dot(normed_two, w_up, preferred_element_type=jnp.float32)).astype(jnp.bfloat16)
    output = first_sum.astype(jnp.float32) + jnp.dot(hidden, w_down, preferred_element_type=jnp.float32)
    return output.reshape(NR, NC, D)

def ocean_core(initial, conv_weight, conv_bias):
    cell_grid = initial.reshape(NR, NC * PACK, OCH)
    for layer_index in range(OLAY):
        padded = jnp.pad(cell_grid, ((1, 1), (0, 0), (0, 0)))
        padded = jnp.concatenate([padded[:, -1:], padded, padded[:, :1]], axis=1)
        accumulated = jnp.zeros((NR * NC * PACK, OCH), jnp.float32)
        for row_step in range(3):
            for col_step in range(3):
                window = padded[row_step:row_step + NR, col_step:col_step + NC * PACK].reshape(-1, OCH)
                accumulated = accumulated + jnp.dot(window, conv_weight[layer_index, row_step, col_step], preferred_element_type=jnp.float32)
        activated = jax.nn.gelu(accumulated.reshape(NR, NC * PACK, OCH) + conv_bias[layer_index])
        cell_grid = (cell_grid.astype(jnp.float32) + activated).astype(jnp.bfloat16)
    return cell_grid.reshape(NR, NC, D).astype(jnp.float32)

def reference(state_field, sea_mask, w_qkv, w_attn_out, w_up, w_down, conv_weight, conv_bias, w_surface, w_forcing, regrid_blocks, routes, dest_entry, block_index):
    sea_factor = sea_mask.astype(jnp.bfloat16)[:, :, None]
    starts = (state_field[0], state_field[1] * sea_factor)
    surfaces = [jnp.dot(blocked(starts[component]), w_surface[component], preferred_element_type=jnp.float32).astype(jnp.bfloat16) for component in range(2)]
    injects = []
    for receiver in range(2):
        source = 1 - receiver
        block_table = regrid_blocks[source].transpose(1, 0, 2).reshape(SFEAT, NBLK * SFEAT)
        spread = jnp.dot(surfaces[source], block_table, preferred_element_type=jnp.float32).reshape(-1, NBLK, SFEAT)
        link_blocks = block_index[source].reshape(-1, TOP)
        selector = (link_blocks[:, :, None] == jnp.arange(NBLK, dtype=jnp.int32)[None, None, :]).astype(jnp.float32)
        link_rows = jnp.einsum('rbs,rtb->rts', spread, selector, precision=lax.Precision.HIGHEST)
        segment_ids = (routes[source].reshape(-1) * ENTRY + dest_entry[source].reshape(-1)).astype(jnp.int32)
        summed = jax.ops.segment_sum(link_rows.reshape(-1, SFEAT), segment_ids, num_segments=GROUP * ENTRY)
        forcing = summed.astype(jnp.bfloat16)
        injects.append(unblocked(jnp.dot(forcing, w_forcing[receiver], preferred_element_type=jnp.float32)))
    core_air = atmosphere_core(starts[0], w_qkv, w_attn_out, w_up, w_down)
    core_water = ocean_core(starts[1], conv_weight, conv_bias)
    new_air = (core_air + injects[0]).astype(jnp.bfloat16)
    new_water = ((core_water + injects[1]) * sea_factor.astype(jnp.float32)).astype(jnp.bfloat16)
    return jnp.stack([new_air, new_water])
```

```python
import functools

import jax
import jax.numpy as jnp
from jax import lax
from jax.experimental import pallas as pl
from jax.experimental.pallas import tpu as pltpu
from jax.sharding import PartitionSpec as P

HEAD = 64
OCH = 128
PACK = 6
WIN = 8
MARGIN = WIN // 2
EPSILON = 1e-05
RADIX = 32
COLPAD = 48
LABEL_ROWS = 16
VMEM_LIMIT = 56 * 1024 * 1024
F32 = jnp.float32
BF16 = jnp.bfloat16
VMEM = pltpu.VMEM
NT = (((1,), (1,)), ((), ()))


def normalize(values):
    average = jnp.mean(values, axis=-1, keepdims=True)
    centred = values - average
    spread = jnp.mean(centred * centred, axis=-1, keepdims=True)
    return centred * lax.rsqrt(spread + EPSILON)


def gelu(x):
    return 0.5 * x * (1.0 + jnp.tanh(0.7978845608028654 * (x + 0.044715 * (x * x * x))))


def iota(shape, dim):
    return lax.broadcasted_iota(jnp.int32, shape, dim)


def onehot(mask):
    return jnp.where(mask, 1.0, 0.0).astype(BF16)


def pack_kernel(surf_ref, table_ref, kind_ref, where_ref, out_ref, links_ref):
    groups, padded_cap, feat = out_ref.shape
    cap = padded_cap - LABEL_ROWS
    entries = surf_ref.shape[0]
    routes = [where_ref[t : t + 1, :] for t in range(2)]
    device = iota((groups, entries), 0)
    match = [jnp.where(device == route, 1.0, 0.0) for route in routes]
    earlier = onehot(iota((entries, entries), 0) < iota((entries, entries), 1))
    counts = jnp.dot((match[0] + match[1]).astype(BF16), earlier, preferred_element_type=F32)
    position, label = [], []
    for t in range(2):
        slot = jnp.sum(match[t] * counts, axis=0, keepdims=True).astype(jnp.int32)
        position.append(routes[t] * cap + slot)
        value = where_ref[2 + t : 3 + t, :] + 1
        high = (value // RADIX).astype(F32)
        low = (value % RADIX).astype(F32)
        row = iota((LABEL_ROWS, entries), 0)
        label.append(jnp.where(row == 0, high, jnp.where(row == 1, low, 0.0)).astype(BF16))
    surf = surf_ref[...]
    spread = [
        jnp.dot(surf, table_ref[b], preferred_element_type=F32) for b in range(table_ref.shape[0])
    ]
    for t in range(2):
        kind = kind_ref[:, t : t + 1]
        total = jnp.where(kind == 0, spread[0], 0.0)
        for b in range(1, len(spread)):
            total = jnp.where(kind == b, spread[b], total)
        links_ref[t * entries : (t + 1) * entries, :] = total.astype(BF16)

    def body(g, carry):
        spot = iota((cap, entries), 0) + g * cap
        pick = jnp.concatenate([onehot(spot == position[t]) for t in range(2)], axis=1)
        rows = jnp.dot(pick, links_ref[...], preferred_element_type=F32)
        out_ref[g, 0:cap, :] = rows.astype(BF16)
        labels = lax.dot_general(
            jnp.concatenate(label, axis=1), pick, NT, preferred_element_type=F32
        ).astype(BF16)
        out_ref[g, cap:padded_cap, :] = jnp.zeros((LABEL_ROWS, feat), BF16)
        out_ref[g, cap:padded_cap, 0:cap] = labels
        return carry

    lax.fori_loop(0, groups, body, 0)


def finish_kernel(got_ref, core_ref, wf_ref, sea_ref, out_ref):
    groups, padded_cap, feat = got_ref.shape
    cap = padded_cap - LABEL_ROWS
    entries = core_ref.shape[0]
    step = 256
    labels = []
    for g in range(groups):
        both = got_ref[g, cap:padded_cap, 0:cap].astype(F32)
        labels.append((both[0:1] * RADIX + both[1:2] - 1.0).astype(jnp.int32))

    for i in range(entries // step):
        entry = iota((step, cap), 0) + i * step
        total = jnp.zeros((step, feat), F32)
        for g in range(groups):
            total = total + jnp.dot(
                onehot(entry == labels[g]), got_ref[g, 0:cap, :], preferred_element_type=F32
            )
        inject = jnp.dot(total.astype(BF16), wf_ref[...], preferred_element_type=F32)
        rows = slice(i * step, (i + 1) * step)
        out_ref[rows, :] = ((core_ref[rows, :] + inject) * sea_ref[rows, :]).astype(BF16)


def conv_kernel(place_ref, x_ref, w_ref, b_ref, out_ref, even_ref, odd_ref):
    ext_rows, cols, width = x_ref.shape
    layers = w_ref.shape[0]
    height, breadth, _ = out_ref.shape
    first_row, grid_rows = place_ref[0], place_ref[1]
    pairs = PACK // 2

    def put(dst, row, first, last):
        left = pltpu.roll(last.astype(F32), 1, 0).astype(BF16)
        right = pltpu.roll(first.astype(F32), cols - 1, 0).astype(BF16)
        dst[row, :, 0:OCH] = left
        dst[row, :, OCH + width :] = right

    def fill(r, carry):
        row = x_ref[r]
        even_ref[r, :, OCH : OCH + width] = row
        put(even_ref, r, row[:, 0:OCH], row[:, width - OCH :])
        return carry

    lax.fori_loop(MARGIN - layers, ext_rows - MARGIN + layers, fill, 0)
    block = 2
    for layer in range(layers):
        src, dst = (even_ref, odd_ref) if layer % 2 == 0 else (odd_ref, even_ref)
        start = MARGIN - layers + layer + 1
        steps = (ext_rows - 2 * start) // block
        bias = b_ref[layer : layer + 1, :]

        def body(i, carry, layer=layer, src=src, dst=dst, start=start, bias=bias):
            base = start + i * block
            parts = []
            for dy in range(3):
                rows = src[pl.ds(base - 1 + dy, block)].reshape(block * cols, -1)
                parts.append(
                    jnp.concatenate(
                        [rows[:, 256 * j : 256 * j + 512] for j in range(pairs)], axis=0
                    )
                )
            total = jnp.dot(
                jnp.concatenate(parts, axis=1), w_ref[layer], preferred_element_type=F32
            )
            active = gelu(total + bias)
            for k in range(block):
                row = base + k
                at = first_row + row
                inside = (at >= 0) & (at < grid_rows)
                cells = []
                for j in range(pairs):
                    begin = (j * block + k) * cols
                    lanes = slice(OCH + 256 * j, OCH + 256 * j + 256)
                    old = src[row, :, lanes].astype(F32)
                    new = jnp.where(inside, old + active[begin : begin + cols], 0.0)
                    cells.append(new.astype(BF16))
                    if layer < layers - 1:
                        dst[row, :, lanes] = cells[-1]
                    else:
                        out_ref[row - MARGIN, :, 256 * j : 256 * j + 256] = (
                            cells[-1][0:breadth].astype(F32)
                        )
                if layer < layers - 1:
                    put(dst, row, cells[0][:, 0:OCH], cells[-1][:, OCH:])
            return carry

        lax.fori_loop(0, steps, body, 0)


def attend_kernel(
    place_ref, x_ref, own_ref, wqkv_ref, wo_ref, wu_ref, wd_ref, out_ref,
    normed_ref, qkv_ref, wide_ref, att_ref,
):
    ext_rows, ext_cols, width = x_ref.shape
    win_rows, win_cols = ext_rows // WIN, ext_cols // WIN
    size = WIN * WIN
    height, breadth = ext_rows - 2 * MARGIN, ext_cols - 2 * MARGIN
    first_row, grid_rows = place_ref[0], place_ref[1]
    heads = 4
    lanes = heads * HEAD
    lane_head = iota((size, lanes), 1) // HEAD
    ones = onehot(iota((lanes, lanes), 0) // HEAD == iota((lanes, lanes), 1) // HEAD)

    def window_row(wr, carry):
        for wc in range(win_cols):
            tokens = jnp.concatenate(
                [
                    x_ref[wr * WIN + r, wc * WIN : (wc + 1) * WIN, :].astype(F32)
                    for r in range(WIN)
                ],
                axis=0,
            )
            normed_ref[wc * size : (wc + 1) * size, :] = normalize(tokens).astype(BF16)
        part = width
        for c in range(3):
            qkv = jnp.dot(
                normed_ref[...], wqkv_ref[:, c * part : (c + 1) * part], preferred_element_type=F32
            )
            if c == 0:
                qkv = qkv * HEAD ** (-0.5)
            qkv_ref[:, c * part : (c + 1) * part] = qkv.astype(BF16)
        key_row = first_row + wr * WIN + (iota((1, lanes), 1) % HEAD) // WIN
        key_ok = (key_row >= 0) & (key_row < grid_rows)

        def window(wc, carry):
            rows = pl.ds(wc * size, size)
            for group in range(width // lanes):
                at = group * lanes
                q = qkv_ref[rows, at : at + lanes]
                k = qkv_ref[rows, width + at : width + at + lanes]
                v = qkv_ref[rows, 2 * width + at : 2 * width + at + lanes]
                zero = jnp.zeros_like(k)
                ks = jnp.concatenate(
                    [jnp.where(lane_head == h, k, zero) for h in range(heads)], axis=0
                )
                vs = jnp.concatenate(
                    [jnp.where(lane_head == h, v, zero) for h in range(heads)], axis=0
                )
                scores = lax.dot_general(q, ks, NT, preferred_element_type=F32)
                scores = jnp.where(key_ok, scores, -1e30)
                halves = []
                for c in range(heads // 2):
                    s = scores[:, c * 128 : (c + 1) * 128]
                    low = lane_head[:, 0:128] == 0
                    m0 = jnp.max(jnp.where(low, s, -1e30), axis=1, keepdims=True)
                    m1 = jnp.max(jnp.where(low, -1e30, s), axis=1, keepdims=True)
                    halves.append(jnp.exp(s - jnp.where(low, m0, m1)))
                e = jnp.concatenate(halves, axis=1).astype(BF16)
                sums = jnp.dot(e, ones, preferred_element_type=F32)
                got = jnp.dot(e, vs, preferred_element_type=F32) / sums
                for r in range(WIN):
                    wide_ref[
                        wr * WIN + r, pl.ds(pl.multiple_of(wc * WIN, WIN), WIN), at : at + lanes
                    ] = got[r * WIN : (r + 1) * WIN]
            return carry

        lax.fori_loop(0, win_cols, window, 0)
        return carry

    lax.fori_loop(0, win_rows, window_row, 0)

    def gather(r, carry):
        att_ref[pl.ds(pl.multiple_of(r * breadth, breadth), breadth), :] = wide_ref[
            r + MARGIN, MARGIN : MARGIN + breadth, :
        ].astype(BF16)
        return carry

    lax.fori_loop(0, height, gather, 0)
    step = 256
    hid = wu_ref.shape[1]
    chunk = 768

    def mlp(i, carry):
        rows = pl.ds(pl.multiple_of(i * step, step), step)
        projected = jnp.dot(att_ref[rows, :], wo_ref[...], preferred_element_type=F32)
        first = (own_ref[rows, :].astype(F32) + projected).astype(BF16).astype(F32)
        second = normalize(first).astype(BF16)
        total = first
        for c in range(hid // chunk):
            cut = slice(c * chunk, (c + 1) * chunk)
            hidden = gelu(jnp.dot(second, wu_ref[:, cut], preferred_element_type=F32)).astype(BF16)
            total = total + jnp.dot(hidden, wd_ref[cut, :], preferred_element_type=F32)
        out_ref[rows, :] = total
        return carry

    lax.fori_loop(0, height * breadth // step, mlp, 0)


def call(kernel, shape, dtype, args, scratch, flops, smem_first=False):
    specs = [pl.BlockSpec(memory_space=VMEM) for _ in args]
    if smem_first:
        specs[0] = pl.BlockSpec(memory_space=pltpu.SMEM)
    return pl.pallas_call(
        kernel,
        out_shape=jax.ShapeDtypeStruct(shape, dtype),
        in_specs=specs,
        out_specs=pl.BlockSpec(memory_space=VMEM),
        scratch_shapes=scratch,
        compiler_params=pltpu.CompilerParams(vmem_limit_bytes=VMEM_LIMIT),
        cost_estimate=pl.CostEstimate(flops=flops, bytes_accessed=8 << 20, transcendentals=0),
    )(*args)


def pair_weights(conv_weight):
    layers = conv_weight.shape[0]
    zero = jnp.zeros_like(conv_weight[:, :, 0])
    w = [conv_weight[:, :, dx] for dx in range(3)]
    left = jnp.concatenate([w[0], w[1], w[2], zero], axis=2)
    right = jnp.concatenate([zero, w[0], w[1], w[2]], axis=2)
    return jnp.concatenate([left, right], axis=3).reshape(layers, 3 * 4 * OCH, 2 * OCH)


def convolve(extended, place, conv_weight, conv_bias):
    ext_rows, ext_cols, width = extended.shape
    height, breadth = ext_rows - 2 * MARGIN, ext_cols - 2 * MARGIN
    x = jnp.concatenate(
        [
            extended[:, MARGIN:],
            jnp.zeros((ext_rows, COLPAD - ext_cols, width), BF16),
            extended[:, :MARGIN],
        ],
        axis=1,
    )
    bias = jnp.concatenate([conv_bias, conv_bias], axis=1)
    scratch = [VMEM((ext_rows, COLPAD, width + 2 * OCH), BF16)] * 2
    core = call(
        conv_kernel, (height, breadth, width), F32,
        (place, x, pair_weights(conv_weight), bias), scratch, 40 * 10**9, True,
    )
    return core.reshape(height * breadth, width)


def attend(extended, own, place, w_qkv, w_attn_out, w_up, w_down):
    ext_rows, ext_cols, width = extended.shape
    entries = own.shape[0]
    scratch = [
        VMEM((ext_cols * WIN, width), BF16),
        VMEM((ext_cols * WIN, 3 * width), BF16),
        VMEM((ext_rows, ext_cols, width), F32),
        VMEM((entries, width), BF16),
    ]
    return call(
        attend_kernel, (entries, width), F32,
        (place, extended, own, w_qkv, w_attn_out, w_up, w_down), scratch, 60 * 10**9, True,
    )


def pack(surface, table, kind, where, groups, capacity):
    entries, feat = surface.shape
    return call(
        pack_kernel, (groups, capacity + LABEL_ROWS, feat), BF16, (surface, table, kind, where),
        [VMEM((2 * entries, feat), BF16)], 6 * 10**9,
    )


def finish(got, core, w_forcing, sea):
    return call(finish_kernel, core.shape, BF16, (got, core, w_forcing, sea), [], 6 * 10**9)


def padded(x, axis, dim, width, wrap):
    peers, length = (lax.axis_size(axis), x.shape[dim])
    up = [(i, (i + 1) % peers) for i in range(peers if wrap else peers - 1)]
    down = [(j, i) for i, j in up]
    last = lax.slice_in_dim(x, length - width, length, axis=dim)
    first = lax.slice_in_dim(x, 0, width, axis=dim)
    before = lax.ppermute(last, axis, up)
    after = lax.ppermute(first, axis, down)
    return jnp.concatenate([before, x, after], axis=dim)


def local(
    state_field, sea_mask, w_qkv, w_attn_out, w_up, w_down, conv_weight, conv_bias,
    w_surface, w_forcing, regrid_blocks, routes, dest_entry, block_index,
):
    component = lax.axis_index("comp")
    is_ocean = component == 1
    local_state = state_field[0]
    height, breadth, width = local_state.shape
    entries = height * breadth
    groups = lax.axis_size("lat") * lax.axis_size("lon")
    top = routes.shape[-1]
    capacity = 3 * entries * top // (2 * groups)
    sea = jnp.where(is_ocean, sea_mask, 1)
    initial = local_state * sea.astype(BF16)[:, :, None]
    swap = [(0, 1), (1, 0)]
    where = jnp.concatenate(
        [routes.reshape(entries, top).T, dest_entry.reshape(entries, top).T], axis=0
    )
    where = lax.ppermute(where, "comp", swap)
    kind = lax.ppermute(block_index.reshape(entries, top), "comp", swap)
    own = initial.reshape(entries, width)
    surface = jnp.dot(own, w_surface[0], preferred_element_type=F32).astype(BF16)
    surface = lax.ppermute(surface, "comp", swap)
    lon_wide = padded(initial, "lon", 1, MARGIN, True)
    extended = padded(lon_wide, "lat", 0, MARGIN, False)
    table = lax.dynamic_index_in_dim(regrid_blocks, 1 - component, 0, keepdims=False)
    outgoing = pack(surface, table, kind, where, groups, capacity)
    got = lax.all_to_all(outgoing, ("lat", "lon"), split_axis=0, concat_axis=0, tiled=True)
    first_row = lax.axis_index("lat") * height - MARGIN
    grid_rows = height * lax.axis_size("lat")
    place = jnp.stack([first_row, jnp.full_like(first_row, grid_rows)]).astype(jnp.int32)
    core = lax.cond(
        is_ocean,
        lambda ext: convolve(ext, place, conv_weight, conv_bias),
        lambda ext: attend(ext, own, place, w_qkv, w_attn_out, w_up, w_down),
        extended,
    )
    result = finish(got, core, w_forcing[0], sea.astype(F32).reshape(entries, 1))
    return result.reshape(1, height, breadth, width)


def solution(mesh):
    placed = (
        P("comp", "lat", "lon", None), P("lat", "lon"), P(), P(), P(), P(), P(), P(),
        P("comp", None, None), P("comp", None, None), P(),
        P("comp", "lat", "lon", None, None),
        P("comp", "lat", "lon", None, None),
        P("comp", "lat", "lon", None, None),
    )
    return jax.shard_map(
        local, mesh=mesh, in_specs=placed, out_specs=P("comp", "lat", "lon", None), check_vma=False
    )
```

```python
import functools

import jax
import jax.numpy as jnp
from jax import lax
from jax.experimental import pallas as pl
from jax.experimental.pallas import tpu as pltpu
from jax.sharding import PartitionSpec as P

HEAD = 64
OCH = 128
PACK = 6
WIN = 8
MARGIN = WIN // 2
EPSILON = 1e-05
RADIX = 32
SIDE = 16
LABEL_ROWS = 16
VMEM_LIMIT = 56 * 1024 * 1024
F32 = jnp.float32
BF16 = jnp.bfloat16
VMEM = pltpu.VMEM
NT = (((1,), (1,)), ((), ()))


def normalize(values):
    average = jnp.mean(values, axis=-1, keepdims=True)
    centred = values - average
    spread = jnp.mean(centred * centred, axis=-1, keepdims=True)
    return centred * lax.rsqrt(spread + EPSILON)


def gelu(x):
    return 0.5 * x * (1.0 + jnp.tanh(0.7978845608028654 * (x + 0.044715 * (x * x * x))))


def iota(shape, dim):
    return lax.broadcasted_iota(jnp.int32, shape, dim)


def onehot(mask):
    return jnp.where(mask, 1.0, 0.0).astype(BF16)


def pack_kernel(surf_ref, table_ref, kind_ref, where_ref, out_ref, links_ref):
    groups, padded_cap, feat = out_ref.shape
    cap = padded_cap - LABEL_ROWS
    entries = surf_ref.shape[0]
    routes = [where_ref[t : t + 1, :] for t in range(2)]
    device = iota((groups, entries), 0)
    match = [jnp.where(device == route, 1.0, 0.0) for route in routes]
    earlier = onehot(iota((entries, entries), 0) < iota((entries, entries), 1))
    counts = jnp.dot((match[0] + match[1]).astype(BF16), earlier, preferred_element_type=F32)
    position, label = [], []
    for t in range(2):
        slot = jnp.sum(match[t] * counts, axis=0, keepdims=True).astype(jnp.int32)
        position.append(routes[t] * cap + slot)
        value = where_ref[2 + t : 3 + t, :] + 1
        high = (value // RADIX).astype(F32)
        low = (value % RADIX).astype(F32)
        row = iota((LABEL_ROWS, entries), 0)
        label.append(jnp.where(row == 0, high, jnp.where(row == 1, low, 0.0)).astype(BF16))
    surf = surf_ref[...]
    spread = [
        jnp.dot(surf, table_ref[b], preferred_element_type=F32) for b in range(table_ref.shape[0])
    ]
    for t in range(2):
        kind = kind_ref[:, t : t + 1]
        total = jnp.where(kind == 0, spread[0], 0.0)
        for b in range(1, len(spread)):
            total = jnp.where(kind == b, spread[b], total)
        links_ref[t * entries : (t + 1) * entries, :] = total.astype(BF16)

    many = 4

    def body(g, carry):
        spot = iota((many * cap, entries), 0) + g * many * cap
        pick = jnp.concatenate([onehot(spot == position[t]) for t in range(2)], axis=1)
        rows = jnp.dot(pick, links_ref[...], preferred_element_type=F32)
        labels = lax.dot_general(
            jnp.concatenate(label, axis=1), pick, NT, preferred_element_type=F32
        ).astype(BF16)
        for m in range(many):
            cut = slice(m * cap, (m + 1) * cap)
            out_ref[g * many + m, 0:cap, :] = rows[cut].astype(BF16)
            out_ref[g * many + m, cap:padded_cap, :] = jnp.zeros((LABEL_ROWS, feat), BF16)
            out_ref[g * many + m, cap:padded_cap, 0:cap] = labels[:, cut]
        return carry

    lax.fori_loop(0, groups // many, body, 0)


def finish_kernel(got_ref, core_ref, wf_ref, sea_ref, out_ref):
    groups, padded_cap, feat = got_ref.shape
    cap = padded_cap - LABEL_ROWS
    height, breadth, _ = out_ref.shape
    entries = height * breadth
    step = 256
    labels = []
    for g in range(groups):
        both = got_ref[g, cap:padded_cap, 0:cap].astype(F32)
        labels.append((both[0:1] * RADIX + both[1:2] - 1.0).astype(jnp.int32))
    rows = jnp.concatenate([got_ref[g, 0:cap, :] for g in range(groups)], axis=0)
    for i in range(entries // step):
        entry = iota((step, cap), 0) + i * step
        pick = jnp.concatenate([onehot(entry == label) for label in labels], axis=1)
        total = jnp.dot(pick, rows, preferred_element_type=F32)
        inject = jnp.dot(total.astype(BF16), wf_ref[...], preferred_element_type=F32)
        for k in range(step // breadth):
            r = i * (step // breadth) + k
            at = slice(k * breadth, (k + 1) * breadth)
            core = core_ref[r * breadth : (r + 1) * breadth, :]
            out_ref[r] = ((core + inject[at]) * sea_ref[:, r : r + 1]).astype(BF16)


def conv_kernel(
    place_ref, own_ref, side_ref, top_ref, bottom_ref, taps_ref, b_ref, out_ref,
    even_ref, odd_ref, w_ref,
):
    ext_rows, cols, _ = even_ref.shape
    layers = w_ref.shape[0]
    height, breadth, width = out_ref.shape
    for layer in range(layers):
        for dy in range(3):
            for i in range(4):
                for o in range(2):
                    tap = jnp.zeros((OCH, OCH), BF16)
                    if 0 <= i - o <= 2:
                        tap = taps_ref[layer, dy, i - o]
                    at = (4 * dy + i) * OCH
                    w_ref[layer, at : at + OCH, o * OCH : (o + 1) * OCH] = tap
    first_row, grid_rows = place_ref[0], place_ref[1]
    pairs = PACK // 2

    def put(dst, row, first, last):
        left = pltpu.roll(last.astype(F32), 1, 0).astype(BF16)
        right = pltpu.roll(first.astype(F32), cols - 1, 0).astype(BF16)
        dst[row, :, 0:OCH] = left
        dst[row, :, OCH + width :] = right

    def fill(r, row):
        even_ref[r, :, OCH : OCH + width] = row
        put(even_ref, r, row[:, 0:OCH], row[:, width - OCH :])

    def middle(r, carry):
        fill(r + MARGIN, jnp.concatenate([own_ref[r], side_ref[r]], axis=0))
        return carry

    for r in range(MARGIN):
        fill(r, top_ref[r])
        fill(height + MARGIN + r, bottom_ref[r])
    lax.fori_loop(0, height, middle, 0)
    block = 2
    for layer in range(layers):
        src, dst = (even_ref, odd_ref) if layer % 2 == 0 else (odd_ref, even_ref)
        start = MARGIN - layers + layer + 1
        steps = (ext_rows - 2 * start) // block
        bias = jnp.concatenate([b_ref[layer : layer + 1, :]] * 2, axis=1)

        def body(i, carry, layer=layer, src=src, dst=dst, start=start, bias=bias):
            base = start + i * block
            parts = []
            for dy in range(3):
                rows = src[pl.ds(base - 1 + dy, block)].reshape(block * cols, -1)
                parts.append(
                    jnp.concatenate(
                        [rows[:, 256 * j : 256 * j + 512] for j in range(pairs)], axis=0
                    )
                )
            total = jnp.dot(
                jnp.concatenate(parts, axis=1), w_ref[layer], preferred_element_type=F32
            )
            active = gelu(total + bias)
            for k in range(block):
                row = base + k
                at = first_row + row
                inside = (at >= 0) & (at < grid_rows)
                cells = []
                for j in range(pairs):
                    begin = (j * block + k) * cols
                    lanes = slice(OCH + 256 * j, OCH + 256 * j + 256)
                    old = src[row, :, lanes].astype(F32)
                    new = jnp.where(inside, old + active[begin : begin + cols], 0.0)
                    cells.append(new.astype(BF16))
                    if layer < layers - 1:
                        dst[row, :, lanes] = cells[-1]
                    else:
                        out_ref[row - MARGIN, :, 256 * j : 256 * j + 256] = (
                            cells[-1][0:breadth].astype(F32)
                        )
                if layer < layers - 1:
                    put(dst, row, cells[0][:, 0:OCH], cells[-1][:, OCH:])
            return carry

        lax.fori_loop(0, steps, body, 0)


def attend_kernel(
    place_ref, own_ref, side_ref, top_ref, bottom_ref, wqkv_ref, wo_ref, wu_ref, wd_ref, out_ref,
    normed_ref, qkv_ref, wide_ref, att_ref,
):
    ext_rows, _, width = wide_ref.shape
    ext_cols = own_ref.shape[1] + 2 * MARGIN
    win_rows, win_cols = ext_rows // WIN, ext_cols // WIN
    size = WIN * WIN
    height, breadth = ext_rows - 2 * MARGIN, ext_cols - 2 * MARGIN
    first_row, grid_rows = place_ref[0], place_ref[1]

    def fill(r, row):
        wide_ref[r] = pltpu.roll(normalize(row.astype(F32)), MARGIN, 0)

    def middle(r, carry):
        fill(r + MARGIN, jnp.concatenate([own_ref[r], side_ref[r]], axis=0))
        return carry

    for r in range(MARGIN):
        fill(r, top_ref[r])
        fill(height + MARGIN + r, bottom_ref[r])
    lax.fori_loop(0, height, middle, 0)
    heads = 4
    lanes = heads * HEAD
    lane_head = iota((size, lanes), 1) // HEAD
    ones = onehot(iota((lanes, lanes), 0) // HEAD == iota((lanes, lanes), 1) // HEAD)

    def window_row(wr, carry):
        for wc in range(win_cols):
            tokens = jnp.concatenate(
                [
                    wide_ref[wr * WIN + r, wc * WIN : (wc + 1) * WIN, :]
                    for r in range(WIN)
                ],
                axis=0,
            )
            normed_ref[wc * size : (wc + 1) * size, :] = tokens.astype(BF16)
        part = width
        for c in range(3):
            qkv = jnp.dot(
                normed_ref[...], wqkv_ref[:, c * part : (c + 1) * part], preferred_element_type=F32
            )
            if c == 0:
                qkv = qkv * HEAD ** (-0.5)
            qkv_ref[:, c * part : (c + 1) * part] = qkv.astype(BF16)
        key_row = first_row + wr * WIN + (iota((1, lanes), 1) % HEAD) // WIN
        key_ok = (key_row >= 0) & (key_row < grid_rows)

        def window(wc, carry):
            rows = pl.ds(wc * size, size)
            for group in range(width // lanes):
                at = group * lanes
                q = qkv_ref[rows, at : at + lanes]
                k = qkv_ref[rows, width + at : width + at + lanes]
                v = qkv_ref[rows, 2 * width + at : 2 * width + at + lanes]
                zero = jnp.zeros_like(k)
                ks = jnp.concatenate(
                    [jnp.where(lane_head == h, k, zero) for h in range(heads)], axis=0
                )
                vs = jnp.concatenate(
                    [jnp.where(lane_head == h, v, zero) for h in range(heads)], axis=0
                )
                scores = lax.dot_general(q, ks, NT, preferred_element_type=F32)
                scores = jnp.where(key_ok, scores, -1e30)
                halves = []
                for c in range(heads // 2):
                    s = scores[:, c * 128 : (c + 1) * 128]
                    low = lane_head[:, 0:128] == 0
                    m0 = jnp.max(jnp.where(low, s, -1e30), axis=1, keepdims=True)
                    m1 = jnp.max(jnp.where(low, -1e30, s), axis=1, keepdims=True)
                    halves.append(jnp.exp(s - jnp.where(low, m0, m1)))
                e = jnp.concatenate(halves, axis=1).astype(BF16)
                sums = jnp.dot(e, ones, preferred_element_type=F32)
                got = jnp.dot(e, vs, preferred_element_type=F32) / sums
                for r in range(WIN):
                    wide_ref[
                        wr * WIN + r, pl.ds(pl.multiple_of(wc * WIN, WIN), WIN), at : at + lanes
                    ] = got[r * WIN : (r + 1) * WIN]
            return carry

        lax.fori_loop(0, win_cols, window, 0)
        return carry

    lax.fori_loop(0, win_rows, window_row, 0)

    def gather(r, carry):
        att_ref[pl.ds(pl.multiple_of(r * breadth, breadth), breadth), :] = wide_ref[
            r + MARGIN, MARGIN : MARGIN + breadth, :
        ].astype(BF16)
        return carry

    lax.fori_loop(0, height, gather, 0)
    step = 256
    hid = wu_ref.shape[1]
    chunk = 768

    def mlp(i, carry):
        rows = pl.ds(pl.multiple_of(i * step, step), step)
        tokens = own_ref[pl.ds(i * (step // breadth), step // breadth)].reshape(step, width)
        projected = jnp.dot(att_ref[rows, :], wo_ref[...], preferred_element_type=F32)
        first = (tokens.astype(F32) + projected).astype(BF16).astype(F32)
        second = normalize(first).astype(BF16)
        total = first
        for c in range(hid // chunk):
            cut = slice(c * chunk, (c + 1) * chunk)
            hidden = gelu(jnp.dot(second, wu_ref[:, cut], preferred_element_type=F32)).astype(BF16)
            total = total + jnp.dot(hidden, wd_ref[cut, :], preferred_element_type=F32)
        out_ref[rows, :] = total
        return carry

    lax.fori_loop(0, height * breadth // step, mlp, 0)


def call(kernel, shape, dtype, args, scratch, flops, smem_first=False):
    specs = [pl.BlockSpec(memory_space=VMEM) for _ in args]
    if smem_first:
        specs[0] = pl.BlockSpec(memory_space=pltpu.SMEM)
    return pl.pallas_call(
        kernel,
        out_shape=jax.ShapeDtypeStruct(shape, dtype),
        in_specs=specs,
        out_specs=pl.BlockSpec(memory_space=VMEM),
        scratch_shapes=scratch,
        compiler_params=pltpu.CompilerParams(vmem_limit_bytes=VMEM_LIMIT),
        cost_estimate=pl.CostEstimate(flops=flops, bytes_accessed=8 << 20, transcendentals=0),
    )(*args)


def convolve(pieces, place, conv_weight, conv_bias):
    height, breadth, width = pieces[0].shape
    cols = pieces[2].shape[1]
    scratch = [VMEM((height + 2 * MARGIN, cols, width + 2 * OCH), BF16)] * 2
    scratch.append(VMEM((conv_weight.shape[0], 12 * OCH, 2 * OCH), BF16))
    core = call(
        conv_kernel, (height, breadth, width), F32,
        (place, *pieces, conv_weight, conv_bias), scratch, 40 * 10**9, True,
    )
    return core.reshape(height * breadth, width)


def attend(pieces, place, w_qkv, w_attn_out, w_up, w_down):
    height, breadth, width = pieces[0].shape
    cols = pieces[2].shape[1]
    entries, tokens = height * breadth, (breadth + 2 * MARGIN) * WIN
    scratch = [
        VMEM((tokens, width), BF16),
        VMEM((tokens, 3 * width), BF16),
        VMEM((height + 2 * MARGIN, cols, width), F32),
        VMEM((entries, width), BF16),
    ]
    return call(
        attend_kernel, (entries, width), F32,
        (place, *pieces, w_qkv, w_attn_out, w_up, w_down), scratch, 60 * 10**9, True,
    )


def pack(surface, table, kind, where, groups, capacity):
    entries, feat = surface.shape
    return call(
        pack_kernel, (groups, capacity + LABEL_ROWS, feat), BF16, (surface, table, kind, where),
        [VMEM((2 * entries, feat), BF16)], 6 * 10**9,
    )


def finish(got, core, w_forcing, sea):
    shape = (sea.shape[1], sea.shape[0], core.shape[1])
    return call(finish_kernel, shape, BF16, (got, core, w_forcing, sea), [], 6 * 10**9)


def neighbours(x, axis, dim, wrap):
    peers, length = (lax.axis_size(axis), x.shape[dim])
    up = [(i, (i + 1) % peers) for i in range(peers if wrap else peers - 1)]
    down = [(j, i) for i, j in up]
    last = lax.slice_in_dim(x, length - MARGIN, length, axis=dim)
    first = lax.slice_in_dim(x, 0, MARGIN, axis=dim)
    return lax.ppermute(last, axis, up), lax.ppermute(first, axis, down)


def edges(initial):
    height, _, width = initial.shape
    west, east = neighbours(initial, "lon", 1, True)
    gap = jnp.zeros((height, SIDE - 2 * MARGIN, width), BF16)
    return jnp.concatenate([east, gap, west], axis=1)


def local(
    state_field, sea_mask, w_qkv, w_attn_out, w_up, w_down, conv_weight, conv_bias,
    w_surface, w_forcing, regrid_blocks, routes, dest_entry, block_index,
):
    component = lax.axis_index("comp")
    is_ocean = component == 1
    local_state = state_field[0]
    height, breadth, width = local_state.shape
    entries = height * breadth
    groups = lax.axis_size("lat") * lax.axis_size("lon")
    top = routes.shape[-1]
    capacity = 3 * entries * top // (2 * groups)
    sea = jnp.where(is_ocean, sea_mask, 1)
    initial = lax.optimization_barrier(local_state * sea.astype(BF16)[:, :, None])
    swap = [(0, 1), (1, 0)]
    where = jnp.concatenate(
        [routes.reshape(entries, top).T, dest_entry.reshape(entries, top).T], axis=0
    )
    where = lax.ppermute(where, "comp", swap)
    kind = lax.ppermute(block_index.reshape(entries, top), "comp", swap)
    side = edges(initial)
    surface = jnp.dot(initial.reshape(entries, width), w_surface[0], preferred_element_type=F32).astype(BF16)
    surface = lax.ppermute(surface, "comp", swap)
    surface, side = lax.optimization_barrier((surface, side))
    ends = [jnp.concatenate([initial[a], side[a]], axis=1) for a in (slice(0, MARGIN), slice(height - MARGIN, height))]
    top, bottom = neighbours(jnp.concatenate(ends, axis=0), "lat", 0, False)
    table = lax.dynamic_index_in_dim(regrid_blocks, 1 - component, 0, keepdims=False)
    outgoing = pack(surface, table, kind, where, groups, capacity)
    outgoing, top, bottom = lax.optimization_barrier((outgoing, top, bottom))
    got = lax.all_to_all(outgoing, ("lat", "lon"), split_axis=0, concat_axis=0, tiled=True)
    first_row = lax.axis_index("lat") * height - MARGIN
    grid_rows = height * lax.axis_size("lat")
    place = jnp.stack([first_row, jnp.full_like(first_row, grid_rows)]).astype(jnp.int32)
    core = lax.cond(
        is_ocean,
        lambda pieces: convolve(pieces, place, conv_weight, conv_bias),
        lambda pieces: attend(pieces, place, w_qkv, w_attn_out, w_up, w_down),
        (initial, side, top, bottom),
    )
    result = finish(got, core, w_forcing[0], sea.astype(F32).T)
    return result.reshape(1, height, breadth, width)


def solution(mesh):
    placed = (
        P("comp", "lat", "lon", None), P("lat", "lon"), P(), P(), P(), P(), P(), P(),
        P("comp", None, None), P("comp", None, None), P(),
        P("comp", "lat", "lon", None, None),
        P("comp", "lat", "lon", None, None),
        P("comp", "lat", "lon", None, None),
    )
    return jax.shard_map(
        local, mesh=mesh, in_specs=placed, out_specs=P("comp", "lat", "lon", None), check_vma=False
    )
```

```python
import functools

import jax
import jax.numpy as jnp
from jax import lax
from jax.experimental import pallas as pl
from jax.experimental.pallas import tpu as pltpu
from jax.sharding import PartitionSpec as P

HEAD = 64
OCH = 128
PACK = 6
WIN = 8
MARGIN = WIN // 2
EPSILON = 1e-05
RADIX = 32
SIDE = 16
LABEL_ROWS = 16
VMEM_LIMIT = 56 * 1024 * 1024
F32 = jnp.float32
BF16 = jnp.bfloat16
VMEM = pltpu.VMEM
NT = (((1,), (1,)), ((), ()))


def normalize(values):
    average = jnp.mean(values, axis=-1, keepdims=True)
    centred = values - average
    spread = jnp.mean(centred * centred, axis=-1, keepdims=True)
    return centred * lax.rsqrt(spread + EPSILON)


def gelu(x):
    return 0.5 * x * (1.0 + jnp.tanh(0.7978845608028654 * (x + 0.044715 * (x * x * x))))


def iota(shape, dim):
    return lax.broadcasted_iota(jnp.int32, shape, dim)


def onehot(mask):
    return jnp.where(mask, 1.0, 0.0).astype(BF16)


def pack_kernel(surf_ref, table_ref, where_ref, out_ref, links_ref):
    groups, padded_cap, feat = out_ref.shape
    cap = padded_cap - LABEL_ROWS
    entries = surf_ref.shape[0]
    routes = [where_ref[t : t + 1, :] for t in range(2)]
    device = iota((groups, entries), 0)
    match = [jnp.where(device == route, 1.0, 0.0) for route in routes]
    earlier = onehot(iota((entries, entries), 0) < iota((entries, entries), 1))
    counts = jnp.dot((match[0] + match[1]).astype(BF16), earlier, preferred_element_type=F32)
    position, label = [], []
    for t in range(2):
        slot = jnp.sum(match[t] * counts, axis=0, keepdims=True).astype(jnp.int32)
        position.append(routes[t] * cap + slot)
        value = where_ref[2 + t : 3 + t, :] + 1
        high = (value // RADIX).astype(F32)
        low = (value % RADIX).astype(F32)
        row = iota((LABEL_ROWS, entries), 0)
        label.append(jnp.where(row == 0, high, jnp.where(row == 1, low, 0.0)).astype(BF16))
    surf = surf_ref[...]
    kinds = where_ref[...].astype(F32).T
    spread = [
        jnp.dot(surf, table_ref[b], preferred_element_type=F32) for b in range(table_ref.shape[0])
    ]
    for t in range(2):
        kind = kinds[:, 4 + t : 5 + t]
        total = jnp.where(kind == 0, spread[0], 0.0)
        for b in range(1, len(spread)):
            total = jnp.where(kind == b, spread[b], total)
        links_ref[t * entries : (t + 1) * entries, :] = total.astype(BF16)

    many = 4

    def body(g, carry):
        spot = iota((many * cap, entries), 0) + g * many * cap
        pick = jnp.concatenate([onehot(spot == position[t]) for t in range(2)], axis=1)
        rows = jnp.dot(pick, links_ref[...], preferred_element_type=F32)
        labels = lax.dot_general(
            jnp.concatenate(label, axis=1), pick, NT, preferred_element_type=F32
        ).astype(BF16)
        for m in range(many):
            cut = slice(m * cap, (m + 1) * cap)
            out_ref[g * many + m, 0:cap, :] = rows[cut].astype(BF16)
            out_ref[g * many + m, cap:padded_cap, :] = jnp.zeros((LABEL_ROWS, feat), BF16)
            out_ref[g * many + m, cap:padded_cap, 0:cap] = labels[:, cut]
        return carry

    lax.fori_loop(0, groups // many, body, 0)


def finish_kernel(got_ref, core_ref, wf_ref, sea_ref, out_ref):
    groups, padded_cap, feat = got_ref.shape
    cap = padded_cap - LABEL_ROWS
    height, breadth, _ = out_ref.shape
    entries = height * breadth
    step = 256
    labels = []
    for g in range(groups):
        both = got_ref[g, cap:padded_cap, 0:cap].astype(F32)
        labels.append((both[0:1] * RADIX + both[1:2] - 1.0).astype(jnp.int32))
    rows = jnp.concatenate([got_ref[g, 0:cap, :] for g in range(groups)], axis=0)
    for i in range(entries // step):
        entry = iota((step, cap), 0) + i * step
        pick = jnp.concatenate([onehot(entry == label) for label in labels], axis=1)
        total = jnp.dot(pick, rows, preferred_element_type=F32)
        inject = jnp.dot(total.astype(BF16), wf_ref[...], preferred_element_type=F32)
        for k in range(step // breadth):
            r = i * (step // breadth) + k
            at = slice(k * breadth, (k + 1) * breadth)
            core = core_ref[r * breadth : (r + 1) * breadth, :]
            out_ref[r] = ((core + inject[at]) * sea_ref[:, r : r + 1]).astype(BF16)


def conv_kernel(
    place_ref, own_ref, side_ref, top_ref, bottom_ref, taps_ref, b_ref, out_ref,
    even_ref, odd_ref, w_ref,
):
    ext_rows, cols, _ = even_ref.shape
    layers = w_ref.shape[0]
    height, breadth, width = out_ref.shape
    for layer in range(layers):
        for dy in range(3):
            for i in range(4):
                for o in range(2):
                    tap = jnp.zeros((OCH, OCH), BF16)
                    if 0 <= i - o <= 2:
                        tap = taps_ref[layer, dy, i - o]
                    at = (4 * dy + i) * OCH
                    w_ref[layer, at : at + OCH, o * OCH : (o + 1) * OCH] = tap
    first_row, grid_rows = place_ref[0], place_ref[1]
    pairs = PACK // 2

    def put(dst, row, first, last):
        left = pltpu.roll(last.astype(F32), 1, 0).astype(BF16)
        right = pltpu.roll(first.astype(F32), cols - 1, 0).astype(BF16)
        dst[row, :, 0:OCH] = left
        dst[row, :, OCH + width :] = right

    def fill(r, row):
        even_ref[r, :, OCH : OCH + width] = row
        put(even_ref, r, row[:, 0:OCH], row[:, width - OCH :])

    def middle(r, carry):
        fill(r + MARGIN, jnp.concatenate([own_ref[r], side_ref[r]], axis=0))
        return carry

    for r in range(MARGIN):
        fill(r, top_ref[r])
        fill(height + MARGIN + r, bottom_ref[r])
    lax.fori_loop(0, height, middle, 0)
    block = 2
    for layer in range(layers):
        src, dst = (even_ref, odd_ref) if layer % 2 == 0 else (odd_ref, even_ref)
        start = MARGIN - layers + layer + 1
        steps = (ext_rows - 2 * start) // block
        bias = jnp.concatenate([b_ref[layer : layer + 1, :]] * 2, axis=1)

        def body(i, carry, layer=layer, src=src, dst=dst, start=start, bias=bias):
            base = start + i * block
            parts = []
            for dy in range(3):
                rows = src[pl.ds(base - 1 + dy, block)].reshape(block * cols, -1)
                parts.append(
                    jnp.concatenate(
                        [rows[:, 256 * j : 256 * j + 512] for j in range(pairs)], axis=0
                    )
                )
            total = jnp.dot(
                jnp.concatenate(parts, axis=1), w_ref[layer], preferred_element_type=F32
            )
            active = gelu(total + bias)
            for k in range(block):
                row = base + k
                at = first_row + row
                inside = (at >= 0) & (at < grid_rows)
                cells = []
                for j in range(pairs):
                    begin = (j * block + k) * cols
                    lanes = slice(OCH + 256 * j, OCH + 256 * j + 256)
                    old = src[row, :, lanes].astype(F32)
                    new = jnp.where(inside, old + active[begin : begin + cols], 0.0)
                    cells.append(new.astype(BF16))
                    if layer < layers - 1:
                        dst[row, :, lanes] = cells[-1]
                    else:
                        out_ref[row - MARGIN, :, 256 * j : 256 * j + 256] = (
                            cells[-1][0:breadth].astype(F32)
                        )
                if layer < layers - 1:
                    put(dst, row, cells[0][:, 0:OCH], cells[-1][:, OCH:])
            return carry

        lax.fori_loop(0, steps, body, 0)


def attend_kernel(
    place_ref, own_ref, side_ref, top_ref, bottom_ref, wqkv_ref, wo_hbm, wu_hbm, wd_hbm, out_ref,
    normed_ref, qkv_ref, wide_ref, att_ref, wo_ref, wu_ref, wd_ref, sems,
):
    loads = [
        pltpu.make_async_copy(src, dst, sems.at[n])
        for n, (src, dst) in enumerate(((wo_hbm, wo_ref), (wu_hbm, wu_ref), (wd_hbm, wd_ref)))
    ]
    for load in loads:
        load.start()
    ext_rows, _, width = wide_ref.shape
    ext_cols = own_ref.shape[1] + 2 * MARGIN
    win_rows, win_cols = ext_rows // WIN, ext_cols // WIN
    size = WIN * WIN
    height, breadth = ext_rows - 2 * MARGIN, ext_cols - 2 * MARGIN
    first_row, grid_rows = place_ref[0], place_ref[1]

    def fill(r, row):
        wide_ref[r] = pltpu.roll(normalize(row.astype(F32)), MARGIN, 0)

    def middle(r, carry):
        fill(r + MARGIN, jnp.concatenate([own_ref[r], side_ref[r]], axis=0))
        return carry

    for r in range(MARGIN):
        fill(r, top_ref[r])
        fill(height + MARGIN + r, bottom_ref[r])
    lax.fori_loop(0, height, middle, 0)
    heads = 4
    lanes = heads * HEAD
    lane_head = iota((size, lanes), 1) // HEAD
    ones = onehot(iota((lanes, lanes), 0) // HEAD == iota((lanes, lanes), 1) // HEAD)

    def window_row(wr, carry):
        for wc in range(win_cols):
            tokens = jnp.concatenate(
                [
                    wide_ref[wr * WIN + r, wc * WIN : (wc + 1) * WIN, :]
                    for r in range(WIN)
                ],
                axis=0,
            )
            normed_ref[wc * size : (wc + 1) * size, :] = tokens.astype(BF16)
        part = width
        for c in range(3):
            qkv = jnp.dot(
                normed_ref[...], wqkv_ref[:, c * part : (c + 1) * part], preferred_element_type=F32
            )
            if c == 0:
                qkv = qkv * HEAD ** (-0.5)
            qkv_ref[:, c * part : (c + 1) * part] = qkv.astype(BF16)
        key_row = first_row + wr * WIN + (iota((1, lanes), 1) % HEAD) // WIN
        key_ok = (key_row >= 0) & (key_row < grid_rows)

        def window(wc, carry):
            rows = pl.ds(wc * size, size)
            for group in range(width // lanes):
                at = group * lanes
                q = qkv_ref[rows, at : at + lanes]
                k = qkv_ref[rows, width + at : width + at + lanes]
                v = qkv_ref[rows, 2 * width + at : 2 * width + at + lanes]
                zero = jnp.zeros_like(k)
                ks = jnp.concatenate(
                    [jnp.where(lane_head == h, k, zero) for h in range(heads)], axis=0
                )
                vs = jnp.concatenate(
                    [jnp.where(lane_head == h, v, zero) for h in range(heads)], axis=0
                )
                scores = lax.dot_general(q, ks, NT, preferred_element_type=F32)
                scores = jnp.where(key_ok, scores, -1e30)
                halves = []
                for c in range(heads // 2):
                    s = scores[:, c * 128 : (c + 1) * 128]
                    low = lane_head[:, 0:128] == 0
                    m0 = jnp.max(jnp.where(low, s, -1e30), axis=1, keepdims=True)
                    m1 = jnp.max(jnp.where(low, -1e30, s), axis=1, keepdims=True)
                    halves.append(jnp.exp(s - jnp.where(low, m0, m1)))
                e = jnp.concatenate(halves, axis=1).astype(BF16)
                sums = jnp.dot(e, ones, preferred_element_type=F32)
                got = jnp.dot(e, vs, preferred_element_type=F32) / sums
                for r in range(WIN):
                    wide_ref[
                        wr * WIN + r, pl.ds(pl.multiple_of(wc * WIN, WIN), WIN), at : at + lanes
                    ] = got[r * WIN : (r + 1) * WIN]
            return carry

        lax.fori_loop(0, win_cols, window, 0, unroll=True)
        return carry

    lax.fori_loop(0, win_rows, window_row, 0)

    def gather(r, carry):
        att_ref[pl.ds(pl.multiple_of(r * breadth, breadth), breadth), :] = wide_ref[
            r + MARGIN, MARGIN : MARGIN + breadth, :
        ].astype(BF16)
        return carry

    lax.fori_loop(0, height, gather, 0)
    for load in loads:
        load.wait()
    step = 512
    hid = wu_ref.shape[1]
    chunk = 768

    def mlp(i, carry):
        rows = pl.ds(pl.multiple_of(i * step, step), step)
        tokens = own_ref[pl.ds(i * (step // breadth), step // breadth)].reshape(step, width)
        projected = jnp.dot(att_ref[rows, :], wo_ref[...], preferred_element_type=F32)
        first = (tokens.astype(F32) + projected).astype(BF16).astype(F32)
        second = normalize(first).astype(BF16)
        total = first
        for c in range(hid // chunk):
            cut = slice(c * chunk, (c + 1) * chunk)
            hidden = gelu(jnp.dot(second, wu_ref[:, cut], preferred_element_type=F32)).astype(BF16)
            total = total + jnp.dot(hidden, wd_ref[cut, :], preferred_element_type=F32)
        out_ref[rows, :] = total
        return carry

    lax.fori_loop(0, height * breadth // step, mlp, 0)


def call(kernel, shape, dtype, args, scratch, flops, smem_first=False, left=0):
    specs = [pl.BlockSpec(memory_space=VMEM) for _ in args]
    if smem_first:
        specs[0] = pl.BlockSpec(memory_space=pltpu.SMEM)
    for n in range(len(args) - left, len(args)):
        specs[n] = pl.BlockSpec(memory_space=pl.ANY)
    return pl.pallas_call(
        kernel,
        out_shape=jax.ShapeDtypeStruct(shape, dtype),
        in_specs=specs,
        out_specs=pl.BlockSpec(memory_space=VMEM),
        scratch_shapes=scratch,
        compiler_params=pltpu.CompilerParams(vmem_limit_bytes=VMEM_LIMIT),
        cost_estimate=pl.CostEstimate(flops=flops, bytes_accessed=8 << 20, transcendentals=0),
    )(*args)


def convolve(pieces, place, conv_weight, conv_bias):
    height, breadth, width = pieces[0].shape
    cols = pieces[2].shape[1]
    scratch = [VMEM((height + 2 * MARGIN, cols, width + 2 * OCH), BF16)] * 2
    scratch.append(VMEM((conv_weight.shape[0], 12 * OCH, 2 * OCH), BF16))
    core = call(
        conv_kernel, (height, breadth, width), F32,
        (place, *pieces, conv_weight, conv_bias), scratch, 40 * 10**9, True,
    )
    return core.reshape(height * breadth, width)


def attend(pieces, place, w_qkv, w_attn_out, w_up, w_down):
    height, breadth, width = pieces[0].shape
    cols = pieces[2].shape[1]
    entries, tokens = height * breadth, (breadth + 2 * MARGIN) * WIN
    scratch = [
        VMEM((tokens, width), BF16),
        VMEM((tokens, 3 * width), BF16),
        VMEM((height + 2 * MARGIN, cols, width), F32),
        VMEM((entries, width), BF16),
        VMEM(w_attn_out.shape, BF16),
        VMEM(w_up.shape, BF16),
        VMEM(w_down.shape, BF16),
        pltpu.SemaphoreType.DMA((3,)),
    ]
    return call(
        attend_kernel, (entries, width), F32,
        (place, *pieces, w_qkv, w_attn_out, w_up, w_down), scratch, 60 * 10**9, True, 3,
    )


def pack(surface, table, where, groups, capacity):
    entries, feat = surface.shape
    return call(
        pack_kernel, (groups, capacity + LABEL_ROWS, feat), BF16, (surface, table, where),
        [VMEM((2 * entries, feat), BF16)], 6 * 10**9,
    )


def finish(got, core, w_forcing, sea):
    shape = (sea.shape[1], sea.shape[0], core.shape[1])
    return call(finish_kernel, shape, BF16, (got, core, w_forcing, sea), [], 6 * 10**9)


def neighbours(x, axis, dim, wrap):
    peers, length = (lax.axis_size(axis), x.shape[dim])
    up = [(i, (i + 1) % peers) for i in range(peers if wrap else peers - 1)]
    down = [(j, i) for i, j in up]
    last = lax.slice_in_dim(x, length - MARGIN, length, axis=dim)
    first = lax.slice_in_dim(x, 0, MARGIN, axis=dim)
    return lax.ppermute(last, axis, up), lax.ppermute(first, axis, down)


def edges(initial):
    height, _, width = initial.shape
    west, east = neighbours(initial, "lon", 1, True)
    gap = jnp.zeros((height, SIDE - 2 * MARGIN, width), BF16)
    return jnp.concatenate([east, gap, west], axis=1)


def local(
    state_field, sea_mask, w_qkv, w_attn_out, w_up, w_down, conv_weight, conv_bias,
    w_surface, w_forcing, regrid_blocks, routes, dest_entry, block_index,
):
    component = lax.axis_index("comp")
    is_ocean = component == 1
    local_state = state_field[0]
    height, breadth, width = local_state.shape
    entries = height * breadth
    groups = lax.axis_size("lat") * lax.axis_size("lon")
    top = routes.shape[-1]
    capacity = 3 * entries * top // (2 * groups)
    sea = jnp.where(is_ocean, sea_mask, 1)
    initial = lax.optimization_barrier(local_state * sea.astype(BF16)[:, :, None])
    swap = [(0, 1), (1, 0)]
    where = jnp.concatenate(
        [a.reshape(entries, top).T for a in (routes, dest_entry, block_index, block_index)], axis=0
    )
    where = lax.ppermute(where, "comp", swap)
    side = edges(initial)
    surface = jnp.dot(initial.reshape(entries, width), w_surface[0], preferred_element_type=F32).astype(BF16)
    surface = lax.ppermute(surface, "comp", swap)
    surface, side = lax.optimization_barrier((surface, side))
    ends = [jnp.concatenate([initial[a], side[a]], axis=1) for a in (slice(0, MARGIN), slice(height - MARGIN, height))]
    top, bottom = neighbours(jnp.concatenate(ends, axis=0), "lat", 0, False)
    table = lax.dynamic_index_in_dim(regrid_blocks, 1 - component, 0, keepdims=False)
    outgoing = pack(surface, table, where, groups, capacity)
    outgoing, top, bottom = lax.optimization_barrier((outgoing, top, bottom))
    got = lax.all_to_all(outgoing, ("lat", "lon"), split_axis=0, concat_axis=0, tiled=True)
    first_row = lax.axis_index("lat") * height - MARGIN
    grid_rows = height * lax.axis_size("lat")
    place = jnp.stack([first_row, jnp.full_like(first_row, grid_rows)]).astype(jnp.int32)
    core = lax.cond(
        is_ocean,
        lambda pieces: convolve(pieces, place, conv_weight, conv_bias),
        lambda pieces: attend(pieces, place, w_qkv, w_attn_out, w_up, w_down),
        (initial, side, top, bottom),
    )
    result = finish(got, core, w_forcing[0], sea.astype(F32).T)
    return result.reshape(1, height, breadth, width)


def solution(mesh):
    placed = (
        P("comp", "lat", "lon", None), P("lat", "lon"), P(), P(), P(), P(), P(), P(),
        P("comp", None, None), P("comp", None, None), P(),
        P("comp", "lat", "lon", None, None),
        P("comp", "lat", "lon", None, None),
        P("comp", "lat", "lon", None, None),
    )
    return jax.shard_map(
        local, mesh=mesh, in_specs=placed, out_specs=P("comp", "lat", "lon", None), check_vma=False
    )
```

```python
import functools

import jax
import jax.numpy as jnp
from jax import lax
from jax.experimental import pallas as pl
from jax.experimental.pallas import tpu as pltpu
from jax.sharding import PartitionSpec as P

HEAD = 64
OCH = 128
PACK = 6
WIN = 8
MARGIN = WIN // 2
EPSILON = 1e-05
RADIX = 32
SIDE = 16
LABEL_ROWS = 16
VMEM_LIMIT = 56 * 1024 * 1024
F32 = jnp.float32
BF16 = jnp.bfloat16
VMEM = pltpu.VMEM
NT = (((1,), (1,)), ((), ()))


def normalize(values):
    average = jnp.mean(values, axis=-1, keepdims=True)
    centred = values - average
    spread = jnp.mean(centred * centred, axis=-1, keepdims=True)
    return centred * lax.rsqrt(spread + EPSILON)


def gelu(x):
    return 0.5 * x * (1.0 + jnp.tanh(0.7978845608028654 * (x + 0.044715 * (x * x * x))))


def iota(shape, dim):
    return lax.broadcasted_iota(jnp.int32, shape, dim)


def onehot(mask):
    return jnp.where(mask, 1.0, 0.0).astype(BF16)


def pack_kernel(surf_ref, table_ref, where_ref, out_ref, links_ref):
    groups, padded_cap, feat = out_ref.shape
    cap = padded_cap - LABEL_ROWS
    entries = surf_ref.shape[0]
    routes = [where_ref[t : t + 1, :] for t in range(2)]
    device = iota((groups, entries), 0)
    match = [jnp.where(device == route, 1.0, 0.0) for route in routes]
    earlier = onehot(iota((entries, entries), 0) < iota((entries, entries), 1))
    counts = jnp.dot((match[0] + match[1]).astype(BF16), earlier, preferred_element_type=F32)
    position, label = [], []
    for t in range(2):
        slot = jnp.sum(match[t] * counts, axis=0, keepdims=True).astype(jnp.int32)
        position.append(routes[t] * cap + slot)
        value = where_ref[2 + t : 3 + t, :] + 1
        high = (value // RADIX).astype(F32)
        low = (value % RADIX).astype(F32)
        row = iota((LABEL_ROWS, entries), 0)
        label.append(jnp.where(row == 0, high, jnp.where(row == 1, low, 0.0)).astype(BF16))
    surf = surf_ref[...]
    kinds = where_ref[...].astype(F32).T
    spread = [
        jnp.dot(surf, table_ref[b], preferred_element_type=F32) for b in range(table_ref.shape[0])
    ]
    for t in range(2):
        kind = kinds[:, 4 + t : 5 + t]
        total = jnp.where(kind == 0, spread[0], 0.0)
        for b in range(1, len(spread)):
            total = jnp.where(kind == b, spread[b], total)
        links_ref[t * entries : (t + 1) * entries, :] = total.astype(BF16)

    many = 8

    def body(g, carry):
        spot = iota((many * cap, entries), 0) + g * many * cap
        pick = jnp.concatenate([onehot(spot == position[t]) for t in range(2)], axis=1)
        rows = jnp.dot(pick, links_ref[...], preferred_element_type=F32)
        labels = lax.dot_general(
            jnp.concatenate(label, axis=1), pick, NT, preferred_element_type=F32
        ).astype(BF16)
        for m in range(many):
            cut = slice(m * cap, (m + 1) * cap)
            out_ref[g * many + m, 0:cap, :] = rows[cut].astype(BF16)
            out_ref[g * many + m, cap:padded_cap, :] = jnp.zeros((LABEL_ROWS, feat), BF16)
            out_ref[g * many + m, cap:padded_cap, 0:cap] = labels[:, cut]
        return carry

    lax.fori_loop(0, groups // many, body, 0)


def finish_kernel(got_ref, core_ref, wf_ref, sea_ref, out_ref):
    groups, padded_cap, feat = got_ref.shape
    cap = padded_cap - LABEL_ROWS
    height, breadth, _ = out_ref.shape
    entries = height * breadth
    step = 512
    labels = []
    for g in range(groups):
        both = got_ref[g, cap:padded_cap, 0:cap].astype(F32)
        labels.append((both[0:1] * RADIX + both[1:2] - 1.0).astype(jnp.int32))
    rows = jnp.concatenate([got_ref[g, 0:cap, :] for g in range(groups)], axis=0)
    for i in range(entries // step):
        entry = iota((step, cap), 0) + i * step
        pick = jnp.concatenate([onehot(entry == label) for label in labels], axis=1)
        total = jnp.dot(pick, rows, preferred_element_type=F32)
        inject = jnp.dot(total.astype(BF16), wf_ref[...], preferred_element_type=F32)
        for k in range(step // breadth):
            r = i * (step // breadth) + k
            at = slice(k * breadth, (k + 1) * breadth)
            core = core_ref[r * breadth : (r + 1) * breadth, :]
            out_ref[r] = ((core + inject[at]) * sea_ref[:, r : r + 1]).astype(BF16)


def conv_kernel(
    place_ref, own_ref, side_ref, top_ref, bottom_ref, taps_ref, b_ref, out_ref,
    even_ref, odd_ref, w_ref,
):
    ext_rows, cols, _ = even_ref.shape
    layers = w_ref.shape[0]
    height, breadth, width = out_ref.shape
    for layer in range(layers):
        for dy in range(3):
            for i in range(4):
                for o in range(2):
                    tap = jnp.zeros((OCH, OCH), BF16)
                    if 0 <= i - o <= 2:
                        tap = taps_ref[layer, dy, i - o]
                    at = (4 * dy + i) * OCH
                    w_ref[layer, at : at + OCH, o * OCH : (o + 1) * OCH] = tap
    first_row, grid_rows = place_ref[0], place_ref[1]
    pairs = PACK // 2

    def put(dst, row, first, last):
        left = pltpu.roll(last.astype(F32), 1, 0).astype(BF16)
        right = pltpu.roll(first.astype(F32), cols - 1, 0).astype(BF16)
        dst[row, :, 0:OCH] = left
        dst[row, :, OCH + width :] = right

    def fill(r, row):
        even_ref[r, :, OCH : OCH + width] = row
        put(even_ref, r, row[:, 0:OCH], row[:, width - OCH :])

    def middle(r, carry):
        fill(r + MARGIN, jnp.concatenate([own_ref[r], side_ref[r]], axis=0))
        return carry

    for r in range(MARGIN):
        fill(r, top_ref[r])
        fill(height + MARGIN + r, bottom_ref[r])
    lax.fori_loop(0, height, middle, 0)
    block = 2
    for layer in range(layers):
        src, dst = (even_ref, odd_ref) if layer % 2 == 0 else (odd_ref, even_ref)
        start = MARGIN - layers + layer + 1
        steps = (ext_rows - 2 * start) // block
        bias = jnp.concatenate([b_ref[layer : layer + 1, :]] * 2, axis=1)

        def body(i, carry, layer=layer, src=src, dst=dst, start=start, bias=bias):
            base = start + i * block
            parts = []
            for dy in range(3):
                rows = src[pl.ds(base - 1 + dy, block)].reshape(block * cols, -1)
                parts.append(
                    jnp.concatenate(
                        [rows[:, 256 * j : 256 * j + 512] for j in range(pairs)], axis=0
                    )
                )
            total = jnp.dot(
                jnp.concatenate(parts, axis=1), w_ref[layer], preferred_element_type=F32
            )
            active = gelu(total + bias)
            for k in range(block):
                row = base + k
                at = first_row + row
                inside = (at >= 0) & (at < grid_rows)
                cells = []
                for j in range(pairs):
                    begin = (j * block + k) * cols
                    lanes = slice(OCH + 256 * j, OCH + 256 * j + 256)
                    old = src[row, :, lanes].astype(F32)
                    new = jnp.where(inside, old + active[begin : begin + cols], 0.0)
                    cells.append(new.astype(BF16))
                    if layer < layers - 1:
                        dst[row, :, lanes] = cells[-1]
                    else:
                        out_ref[row - MARGIN, :, 256 * j : 256 * j + 256] = (
                            cells[-1][0:breadth].astype(F32)
                        )
                if layer < layers - 1:
                    put(dst, row, cells[0][:, 0:OCH], cells[-1][:, OCH:])
            return carry

        lax.fori_loop(0, steps, body, 0)


def attend_kernel(
    place_ref, own_ref, side_ref, top_ref, bottom_ref, wqkv_ref, wo_hbm, wu_hbm, wd_hbm, out_ref,
    normed_ref, qkv_ref, wide_ref, att_ref, wo_ref, wu_ref, wd_ref, sems,
):
    loads = [
        pltpu.make_async_copy(src, dst, sems.at[n])
        for n, (src, dst) in enumerate(((wo_hbm, wo_ref), (wu_hbm, wu_ref), (wd_hbm, wd_ref)))
    ]
    for load in loads:
        load.start()
    ext_rows, _, width = wide_ref.shape
    ext_cols = own_ref.shape[1] + 2 * MARGIN
    win_rows, win_cols = ext_rows // WIN, ext_cols // WIN
    size = WIN * WIN
    height, breadth = ext_rows - 2 * MARGIN, ext_cols - 2 * MARGIN
    first_row, grid_rows = place_ref[0], place_ref[1]

    def fill(r, row):
        wide_ref[r] = pltpu.roll(normalize(row.astype(F32)), MARGIN, 0)

    def middle(r, carry):
        fill(r + MARGIN, jnp.concatenate([own_ref[r], side_ref[r]], axis=0))
        return carry

    for r in range(MARGIN):
        fill(r, top_ref[r])
        fill(height + MARGIN + r, bottom_ref[r])
    lax.fori_loop(0, height, middle, 0)
    heads = 4
    lanes = heads * HEAD
    lane_head = iota((size, lanes), 1) // HEAD
    ones = onehot(iota((lanes, lanes), 0) // HEAD == iota((lanes, lanes), 1) // HEAD)

    def window_row(wr, carry):
        for wc in range(win_cols):
            tokens = jnp.concatenate(
                [
                    wide_ref[wr * WIN + r, wc * WIN : (wc + 1) * WIN, :]
                    for r in range(WIN)
                ],
                axis=0,
            )
            normed_ref[wc * size : (wc + 1) * size, :] = tokens.astype(BF16)
        part = width
        for c in range(3):
            qkv = jnp.dot(
                normed_ref[...], wqkv_ref[:, c * part : (c + 1) * part], preferred_element_type=F32
            )
            if c == 0:
                qkv = qkv * HEAD ** (-0.5)
            qkv_ref[:, c * part : (c + 1) * part] = qkv.astype(BF16)
        key_row = first_row + wr * WIN + (iota((1, lanes), 1) % HEAD) // WIN
        key_ok = (key_row >= 0) & (key_row < grid_rows)

        def window(wc, carry):
            rows = pl.ds(wc * size, size)
            for group in range(width // lanes):
                at = group * lanes
                q = qkv_ref[rows, at : at + lanes]
                k = qkv_ref[rows, width + at : width + at + lanes]
                v = qkv_ref[rows, 2 * width + at : 2 * width + at + lanes]
                zero = jnp.zeros_like(k)
                ks = jnp.concatenate(
                    [jnp.where(lane_head == h, k, zero) for h in range(heads)], axis=0
                )
                vs = jnp.concatenate(
                    [jnp.where(lane_head == h, v, zero) for h in range(heads)], axis=0
                )
                scores = lax.dot_general(q, ks, NT, preferred_element_type=F32)
                scores = jnp.where(key_ok, scores, -1e30)
                halves = []
                for c in range(heads // 2):
                    s = scores[:, c * 128 : (c + 1) * 128]
                    low = lane_head[:, 0:128] == 0
                    m0 = jnp.max(jnp.where(low, s, -1e30), axis=1, keepdims=True)
                    m1 = jnp.max(jnp.where(low, -1e30, s), axis=1, keepdims=True)
                    halves.append(jnp.exp(s - jnp.where(low, m0, m1)))
                e = jnp.concatenate(halves, axis=1).astype(BF16)
                sums = jnp.dot(e, ones, preferred_element_type=F32)
                got = jnp.dot(e, vs, preferred_element_type=F32) / sums
                for r in range(WIN):
                    wide_ref[
                        wr * WIN + r, pl.ds(pl.multiple_of(wc * WIN, WIN), WIN), at : at + lanes
                    ] = got[r * WIN : (r + 1) * WIN]
            return carry

        lax.fori_loop(0, win_cols, window, 0, unroll=True)
        return carry

    lax.fori_loop(0, win_rows, window_row, 0)

    def gather(r, carry):
        att_ref[pl.ds(pl.multiple_of(r * breadth, breadth), breadth), :] = wide_ref[
            r + MARGIN, MARGIN : MARGIN + breadth, :
        ].astype(BF16)
        return carry

    lax.fori_loop(0, height, gather, 0)
    for load in loads:
        load.wait()
    step = 512
    hid = wu_ref.shape[1]
    chunk = 768

    def mlp(i, carry):
        rows = pl.ds(pl.multiple_of(i * step, step), step)
        tokens = own_ref[pl.ds(i * (step // breadth), step // breadth)].reshape(step, width)
        projected = jnp.dot(att_ref[rows, :], wo_ref[...], preferred_element_type=F32)
        first = (tokens.astype(F32) + projected).astype(BF16).astype(F32)
        second = normalize(first).astype(BF16)
        total = first
        for c in range(hid // chunk):
            cut = slice(c * chunk, (c + 1) * chunk)
            hidden = gelu(jnp.dot(second, wu_ref[:, cut], preferred_element_type=F32)).astype(BF16)
            total = total + jnp.dot(hidden, wd_ref[cut, :], preferred_element_type=F32)
        out_ref[rows, :] = total
        return carry

    lax.fori_loop(0, height * breadth // step, mlp, 0)


def call(kernel, shape, dtype, args, scratch, flops, smem_first=False, left=0):
    specs = [pl.BlockSpec(memory_space=VMEM) for _ in args]
    if smem_first:
        specs[0] = pl.BlockSpec(memory_space=pltpu.SMEM)
    for n in range(len(args) - left, len(args)):
        specs[n] = pl.BlockSpec(memory_space=pl.ANY)
    return pl.pallas_call(
        kernel,
        out_shape=jax.ShapeDtypeStruct(shape, dtype),
        in_specs=specs,
        out_specs=pl.BlockSpec(memory_space=VMEM),
        scratch_shapes=scratch,
        compiler_params=pltpu.CompilerParams(vmem_limit_bytes=VMEM_LIMIT),
        cost_estimate=pl.CostEstimate(flops=flops, bytes_accessed=8 << 20, transcendentals=0),
    )(*args)


def convolve(pieces, place, conv_weight, conv_bias):
    height, breadth, width = pieces[0].shape
    cols = pieces[2].shape[1]
    scratch = [VMEM((height + 2 * MARGIN, cols, width + 2 * OCH), BF16)] * 2
    scratch.append(VMEM((conv_weight.shape[0], 12 * OCH, 2 * OCH), BF16))
    core = call(
        conv_kernel, (height, breadth, width), F32,
        (place, *pieces, conv_weight, conv_bias), scratch, 40 * 10**9, True,
    )
    return core.reshape(height * breadth, width)


def attend(pieces, place, w_qkv, w_attn_out, w_up, w_down):
    height, breadth, width = pieces[0].shape
    cols = pieces[2].shape[1]
    entries, tokens = height * breadth, (breadth + 2 * MARGIN) * WIN
    scratch = [
        VMEM((tokens, width), BF16),
        VMEM((tokens, 3 * width), BF16),
        VMEM((height + 2 * MARGIN, cols, width), F32),
        VMEM((entries, width), BF16),
        VMEM(w_attn_out.shape, BF16),
        VMEM(w_up.shape, BF16),
        VMEM(w_down.shape, BF16),
        pltpu.SemaphoreType.DMA((3,)),
    ]
    return call(
        attend_kernel, (entries, width), F32,
        (place, *pieces, w_qkv, w_attn_out, w_up, w_down), scratch, 60 * 10**9, True, 3,
    )


def pack(surface, table, where, groups, capacity):
    entries, feat = surface.shape
    return call(
        pack_kernel, (groups, capacity + LABEL_ROWS, feat), BF16, (surface, table, where),
        [VMEM((2 * entries, feat), BF16)], 6 * 10**9,
    )


def finish(got, core, w_forcing, sea):
    shape = (sea.shape[1], sea.shape[0], core.shape[1])
    return call(finish_kernel, shape, BF16, (got, core, w_forcing, sea), [], 6 * 10**9)


def neighbours(x, axis, dim, wrap):
    peers, length = (lax.axis_size(axis), x.shape[dim])
    up = [(i, (i + 1) % peers) for i in range(peers if wrap else peers - 1)]
    down = [(j, i) for i, j in up]
    last = lax.slice_in_dim(x, length - MARGIN, length, axis=dim)
    first = lax.slice_in_dim(x, 0, MARGIN, axis=dim)
    return lax.ppermute(last, axis, up), lax.ppermute(first, axis, down)


def edges(initial):
    height, _, width = initial.shape
    west, east = neighbours(initial, "lon", 1, True)
    gap = jnp.zeros((height, SIDE - 2 * MARGIN, width), BF16)
    return jnp.concatenate([east, gap, west], axis=1)


def local(
    state_field, sea_mask, w_qkv, w_attn_out, w_up, w_down, conv_weight, conv_bias,
    w_surface, w_forcing, regrid_blocks, routes, dest_entry, block_index,
):
    component = lax.axis_index("comp")
    is_ocean = component == 1
    local_state = state_field[0]
    height, breadth, width = local_state.shape
    entries = height * breadth
    groups = lax.axis_size("lat") * lax.axis_size("lon")
    top = routes.shape[-1]
    capacity = 3 * entries * top // (2 * groups)
    sea = jnp.where(is_ocean, sea_mask, 1)
    initial = lax.optimization_barrier(local_state * sea.astype(BF16)[:, :, None])
    swap = [(0, 1), (1, 0)]
    where = jnp.concatenate(
        [a.reshape(entries, top).T for a in (routes, dest_entry, block_index, block_index)], axis=0
    )
    where = lax.ppermute(where, "comp", swap)
    side = edges(initial)
    surface = jnp.dot(initial.reshape(entries, width), w_surface[0], preferred_element_type=F32).astype(BF16)
    surface = lax.ppermute(surface, "comp", swap)
    surface, side = lax.optimization_barrier((surface, side))
    ends = [jnp.concatenate([initial[a], side[a]], axis=1) for a in (slice(0, MARGIN), slice(height - MARGIN, height))]
    top, bottom = neighbours(jnp.concatenate(ends, axis=0), "lat", 0, False)
    table = lax.dynamic_index_in_dim(regrid_blocks, 1 - component, 0, keepdims=False)
    outgoing = pack(surface, table, where, groups, capacity)
    outgoing, top, bottom = lax.optimization_barrier((outgoing, top, bottom))
    got = lax.all_to_all(outgoing, ("lat", "lon"), split_axis=0, concat_axis=0, tiled=True)
    first_row = lax.axis_index("lat") * height - MARGIN
    grid_rows = height * lax.axis_size("lat")
    place = jnp.stack([first_row, jnp.full_like(first_row, grid_rows)]).astype(jnp.int32)
    core = lax.cond(
        is_ocean,
        lambda pieces: convolve(pieces, place, conv_weight, conv_bias),
        lambda pieces: attend(pieces, place, w_qkv, w_attn_out, w_up, w_down),
        (initial, side, top, bottom),
    )
    result = finish(got, core, w_forcing[0], sea.astype(F32).T)
    return result.reshape(1, height, breadth, width)


def solution(mesh):
    placed = (
        P("comp", "lat", "lon", None), P("lat", "lon"), P(), P(), P(), P(), P(), P(),
        P("comp", None, None), P("comp", None, None), P(),
        P("comp", "lat", "lon", None, None),
        P("comp", "lat", "lon", None, None),
        P("comp", "lat", "lon", None, None),
    )
    return jax.shard_map(
        local, mesh=mesh, in_specs=placed, out_specs=P("comp", "lat", "lon", None), check_vma=False
    )
```
